1024 devices in a mesh: dp: 8 (over z), tensor: 2 (over core), expert: 64 (over x, y).
Axes of the slice: x: 8, y: 8, z: 8, core: 2. Of those that a mesh axis runs over, the one named last changes fastest.
Arguments:
- tokens: bfloat16 [8192, 4096], P('expert', 'dp'), may hold values from -6 to 6
- cotangent: bfloat16 [8192, 4096], P('expert', 'dp'), may hold values from -6 to 6
- routes: int32 [8192, 4], P('expert'), may hold values from 0 to 63, all different within a row; in each aligned block of 128 rows (0 to 127, 128 to 255, ...) at most 10 rows name the same one
- gates: bfloat16 [8192, 4], P('expert'), may hold values from 0.019897461 to 0.5
- w_gate: bfloat16 [64, 4096, 1536], P('expert', 'dp', 'tensor'), may hold values from -0.09375 to 0.09375
- w_up: bfloat16 [64, 4096, 1536], P('expert', 'dp', 'tensor'), may hold values from -0.09375 to 0.09375
- w_down: bfloat16 [64, 1536, 4096], P('expert', 'tensor', 'dp'), may hold values from -0.15625 to 0.15625
Outputs:
- input_grad: bfloat16 [8192, 4096], P('expert', 'dp')
- down_grad: bfloat16 [64, 1536, 4096], P('expert', 'tensor', 'dp')
The draws below stay inside these ranges and needn't reach their ends.
Inputs may be any that keep to these rules, and one draw needn't show every extreme that they name: `routes`: each row names 4 different experts. In each aligned block of 128 rows (the rows of one device) no expert is named by more than 10 rows, a bound that some block reaches.
All inputs are finite; a program needn't handle non-finite values.
Results may differ from the reference program's by a relative error of at most 0.029.
Values may be sent and summed in bfloat16 or wider, within the bound.
A program may use at most 32 MiB of HBM per device.

```python
import math
import jax
import jax.numpy as jnp
import numpy as np
from jax import lax

D = 4096
FF = 1536
TOK_DEV = 128
EXPERTS = 64
TOP = 4
CAP = 10
TOKENS = 8192
N_DP = 8
N_EXPERT = 64


def block_levels(rng, dims, cuts, low, top_value):
    gain = 1.0
    for dim, blocks in cuts:
        heights = jax.random.uniform(jax.random.fold_in(jax.random.fold_in(rng, 6), dim), (blocks,), jnp.float32, low / len(cuts), top_value / len(cuts))
        gain = gain * jnp.repeat(jnp.exp(heights), dims[dim] // blocks).reshape((-1,) + (1,) * (len(dims) - 1 - dim))
    return gain


def deal_out(rng, own, number, rows, amount, top, bound, lean):
    order = jax.random.permutation(rng, amount)
    crowded, common = shares(amount, rows * top, bound, lean, True), shares(amount, rows * top, bound, lean, False)
    places = jnp.arange(amount)

    def named(lengths, rotation):
        used = int((lengths > 0).sum())
        fixed = max(1, used // 4)
        moved = fixed + (places - fixed + rotation * (used - fixed)) % max(1, amount - fixed)
        return jnp.zeros((amount,), jnp.int32).at[order[jnp.where(places < fixed, places, moved)]].set(jnp.asarray(lengths, jnp.int32))

    lengths = jnp.where(number % 4 == 0, named(crowded, number // 4), named(common, number - number // 4 - 1))
    mixed = jax.random.permutation(jax.random.fold_in(own, 3), amount)
    giver, receiver = mixed[0:amount // 2 * 2:2], mixed[1:amount // 2 * 2:2]
    room = jnp.minimum(lengths[giver] - 1, bound - lengths[receiver]) // 2
    room = jnp.where((giver == order[0]) | (receiver == order[0]) | (lengths[receiver] == 0), 0, jnp.maximum(room, 0))
    moved = jax.random.randint(jax.random.fold_in(own, 4), (amount // 2,), 0, 1 << 20) % (room + 1)
    lengths = lengths.at[giver].add(-moved).at[receiver].add(moved)
    members = jnp.searchsorted(jnp.cumsum(lengths), jnp.arange(rows * top), side="right").astype(jnp.int32)
    grid = members.reshape(top, rows).T
    grid = grid[jax.random.permutation(jax.random.fold_in(own, 1), rows)]
    rotation = jax.random.randint(jax.random.fold_in(own, 2), (rows, 1), 0, top)
    return jnp.take_along_axis(grid, (jnp.arange(top)[None, :] + rotation) % top, axis=1)


def shares(number_of, total, bound, skew, full):
    weights = [(1 << 20) // math.isqrt(standing ** skew) + 1 for standing in range(1, number_of + 1)]
    largest = bound if full else min(bound, max(-(-total // number_of), total * weights[0] // sum(weights)))
    least = 1 if total - largest >= number_of - 1 else 0
    holding, surplus = [largest] + [least] * (number_of - 1), total - largest - least * (number_of - 1)
    while surplus > 0:
        candidates = [i for i in range(1, number_of) if holding[i] < largest] or [i for i in range(1, number_of) if holding[i] < bound]
        mass, left = sum([weights[i] for i in candidates]), surplus
        for i in candidates:
            addition = min(bound - holding[i], max(1, left * weights[i] // mass), surplus)
            holding[i] = holding[i] + addition
            surplus = surplus - addition
    return np.array(holding)


def scatter_about(own_key, dims, deviation, limit, shards=(), kind=jnp.bfloat16):
    factor_of = block_levels(own_key, dims, shards, -0.22, 0.18) if shards else 1.0
    entries = jax.random.normal(own_key, dims, jnp.float32) * deviation * factor_of
    return jnp.minimum(jnp.maximum(entries, -limit), limit).astype(kind)


def setup_inputs(seed: int = 0) -> dict:
    key_of = jax.random.split(jax.random.key(seed), 8)
    tokens = scatter_about(key_of[0], (TOKENS, D), 1.0, 6.0, ((0, 64), (1, 8)))
    cotangent = scatter_about(key_of[1], (TOKENS, D), 1.0, 6.0, ((0, 64), (1, 8)))
    routes_keys = jax.random.split(jax.random.fold_in(key_of[2], 1), TOKENS // TOK_DEV)
    routes_turns = jax.random.permutation(jax.random.fold_in(key_of[2], 3), TOKENS // TOK_DEV)
    routes = jax.vmap(lambda own, number: deal_out(jax.random.fold_in(key_of[2], 2), own, number, TOK_DEV, EXPERTS, TOP, CAP, 2))(routes_keys, routes_turns).reshape((TOKENS, TOP))
    gates = jnp.clip(jnp.exp(math.log(0.5) - 3.224016 * jax.random.uniform(key_of[3], (TOKENS, TOP), jnp.float32) ** block_levels(key_of[3], (TOKENS, TOP), ((0, 64),), -0.2, 0.2)), 0.019897461, 0.5).astype(jnp.bfloat16)
    w_gate = scatter_about(key_of[4], (EXPERTS, D, FF), D ** -0.5, 0.09375, ((0, 64), (1, 8), (2, 2)))
    w_up = scatter_about(key_of[5], (EXPERTS, D, FF), D ** -0.5, 0.09375, ((0, 64), (1, 8), (2, 2)))
    w_down = scatter_about(key_of[6], (EXPERTS, FF, D), FF ** -0.5, 0.15625, ((0, 64), (1, 2), (2, 8)))
    return {"tokens": tokens, "cotangent": cotangent, "routes": routes, "gates": gates, "w_gate": w_gate, "w_up": w_up, "w_down": w_down}


def shard_sums(left, right):
    row_total = left.shape[0]
    inner_width = left.shape[1] // N_DP
    partial_value = jnp.einsum("rnd,ndf->nrf", left.reshape(row_total, N_DP, inner_width).astype(jnp.float32), right.reshape(N_DP, inner_width, right.shape[1]).astype(jnp.float32))
    rounded = lax.optimization_barrier(partial_value.astype(jnp.bfloat16))
    return jnp.sum(rounded.astype(jnp.float32), axis=0)


def reference(tokens, cotangent, routes, gates, w_gate, w_up, w_down):
    row_limit = N_EXPERT * CAP
    route_flat = routes.reshape(-1)
    gate_flat = gates.reshape(-1).astype(jnp.float32)
    pair_count = route_flat.shape[0]

    def per_expert(dx_total, expert_id):
        picked = jnp.nonzero(route_flat == expert_id, size=row_limit, fill_value=pair_count)[0].astype(jnp.int32)
        is_valid = picked < pair_count
        safe_pair = jnp.minimum(picked, pair_count - 1).astype(jnp.int32)
        token_id = (safe_pair // TOP).astype(jnp.int32)
        x_rows = jnp.where(is_valid[:, None], tokens[token_id], jnp.zeros((), tokens.dtype))
        dy_rows = jnp.where(is_valid[:, None], cotangent[token_id], jnp.zeros((), cotangent.dtype))
        weight_g = jnp.where(is_valid, gate_flat[safe_pair], jnp.zeros((), jnp.float32))
        gate_proj = w_gate[expert_id]
        up_proj = w_up[expert_id]
        down_proj = w_down[expert_id]
        gate_sum = shard_sums(x_rows, gate_proj)
        up_sum = shard_sums(x_rows, up_proj)
        back_sum = shard_sums(dy_rows, down_proj.T)
        sig_gate = jax.nn.sigmoid(gate_sum)
        silu_val = gate_sum * sig_gate
        d_hidden = weight_g[:, None] * back_sum
        d_up = (d_hidden * silu_val).astype(jnp.bfloat16)
        d_gate = (d_hidden * up_sum * sig_gate * (1.0 + gate_sum * (1.0 - sig_gate))).astype(jnp.bfloat16)
        scaled = (weight_g[:, None] * silu_val * up_sum).astype(jnp.bfloat16)
        dx_rows = jnp.dot(d_gate, gate_proj.T, preferred_element_type=jnp.float32) + jnp.dot(d_up, up_proj.T, preferred_element_type=jnp.float32)
        dx_rows = jnp.where(is_valid[:, None], dx_rows, jnp.zeros((), jnp.float32))
        dx_total = dx_total.at[token_id].add(dx_rows)
        grad_down = jnp.dot(scaled.T, dy_rows, preferred_element_type=jnp.float32).astype(jnp.bfloat16)
        return dx_total, grad_down

    dx_total, down_grad = lax.scan(per_expert, jnp.zeros((TOKENS, D), jnp.float32), jnp.arange(EXPERTS, dtype=jnp.int32))
    return dx_total.astype(jnp.bfloat16), down_grad
```

```python
import functools
import math

import jax
import jax.numpy as jnp
from jax import lax
from jax.experimental import pallas as pl
from jax.experimental.pallas import tpu as pltpu
from jax.sharding import PartitionSpec as P

MESH = pl.DeviceIdType.MESH
F32 = jnp.float32
BF16 = jnp.bfloat16


def dot(a, b, dims=((1,), (0,))):
    return lax.dot_general(a, b, (dims, ((), ())), preferred_element_type=F32)


def kernel(
    c,
    routes_ref, gates_ref, tok_ref, cot_ref, wg_hbm, wu_hbm, wd_hbm,
    dx_ref, dgrad_ref,
    wg, wu, wd, perm, fin, pcomb,
    s1, a1, s2, a2, rows, own, st0, rs, gat, keep, pxo, pxi, rt, ra, r2, rc, res,
    wsem, d1s, d1r, d2s, d2r, cxs, cxr, rss, rsr, ags, agr, pxs, pxr, r1s, r1r, r2s, r2r, fs, fr,
):
    n, nz, cap, tok, top, width, hid = c
    half_z = nz // 2
    total = n * n * cap
    chunk = total // nz
    block = n * cap
    per = nz // n
    hw = width // 2
    hh = hid // 2
    order = [r for pair in zip(range(n // 2, 0, -1), range(n - n // 2, n)) for r in pair]
    order = list(dict.fromkeys(r for r in order if 0 < r < n))

    z = lax.axis_index("dp")
    core = lax.axis_index("tensor")
    me = lax.axis_index("expert")
    mx, my = me // n, lax.rem(me, n)
    first = (1 - core) * mx + core * my
    second = (1 - core) * my + core * mx

    def at_x(p):
        return {"expert": p * n + my}

    def at_y(p):
        return {"expert": mx * n + p}

    def at_first(p):
        return {"expert": (1 - core) * (p * n + my) + core * (mx * n + p)}

    def at_second(p):
        return {"expert": (1 - core) * (mx * n + p) + core * (p * n + my)}

    other = {"tensor": 1 - core}
    z_to = ({"dp": lax.rem(z + 1, nz)}, {"dp": lax.rem(z + nz - 1, nz)})

    def z_off(k):
        return lax.rem(z + k + 2 * nz, nz)

    def span(i, size):
        return pl.ds(pl.multiple_of(i * size, size), size)

    mine = span(core, hw)
    theirs = span(1 - core, hw)

    loads = [
        pltpu.make_async_copy(src, dst, wsem.at[i])
        for i, (src, dst) in enumerate(((wg_hbm, wg), (wu_hbm, wu), (wd_hbm, wd)))
    ]
    for load in loads:
        load.start()

    barrier = pltpu.get_barrier_semaphore()
    peers = [at_x(lax.rem(mx + r, n)) for r in range(1, n)]
    peers += [at_y(lax.rem(my + r, n)) for r in range(1, n)]
    peers += [other, z_to[0], z_to[1]]
    for peer in peers:
        pl.semaphore_signal(barrier, inc=1, device_id=peer, device_id_type=MESH)

    ex = n * n
    e_row = lax.broadcasted_iota(jnp.int32, (ex, 1), 0).astype(F32)
    e_div = jnp.floor((e_row + 0.5) * (1.0 / n))
    e_swap = (e_row - e_div * n) * n + e_div
    core_f = core.astype(F32)
    e_disp = e_row + core_f * (e_swap - e_row)
    s_row = lax.broadcasted_iota(jnp.int32, (total, 1), 0).astype(F32)
    s_exp = jnp.floor((s_row + 0.5) * (1.0 / cap))
    s_rank = s_row - s_exp * cap
    expand = (s_exp == lax.broadcasted_iota(jnp.int32, (total, ex), 1).astype(F32)).astype(BF16)
    earlier = (
        lax.broadcasted_iota(jnp.int32, (tok, tok), 0) < lax.broadcasted_iota(jnp.int32, (tok, tok), 1)
    ).astype(BF16)
    routes = routes_ref[...].astype(F32)
    gates = gates_ref[...].astype(F32)

    def select(names):
        member = jnp.zeros((ex, tok), F32)
        weight = jnp.zeros((ex, tok), F32)
        for k in range(top):
            hit = routes[k : k + 1, :] == names
            member = member + jnp.where(hit, 1.0, 0.0)
            weight = weight + jnp.where(hit, gates[k : k + 1, :], 0.0)
        rank = dot(member.astype(BF16), earlier)
        placed = (member * (rank + 1.0)).astype(BF16)
        return dot(expand, placed) == s_rank + 1.0, weight

    picked, weight = select(e_disp)
    chosen = jnp.where(picked, 1.0, 0.0).astype(BF16)
    weighted = jnp.where(picked, dot(expand, weight.astype(BF16)), 0.0).astype(BF16)
    s1[0] = dot(chosen, tok_ref[:, mine]).astype(BF16)

    pl.semaphore_wait(barrier, len(peers))

    def exchange(src, dst, ssem, rsem, here, where):
        out = []
        for r in order:
            peer = lax.rem(here + r, n)
            out.append(
                pltpu.make_async_remote_copy(
                    src_ref=src.at[span(peer, block), :],
                    dst_ref=dst.at[span(here, block), :],
                    send_sem=ssem.at[r],
                    recv_sem=rsem.at[r],
                    device_id=where(peer),
                    device_id_type=MESH,
                )
            )
        return out

    pending = []

    def go(copies):
        for copy in copies:
            copy.start()
            pending.append(copy)

    d1 = [exchange(s1.at[i], a1.at[i], d1s.at[i], d1r.at[i], first, at_first) for i in range(2)]
    d2 = [exchange(s2.at[i], a2.at[i], d2s.at[i], d2r.at[i], second, at_second) for i in range(2)]

    go(d1[0])
    a1[0, span(first, block), :] = s1[0, span(first, block), :]
    s1[1] = dot(weighted, cot_ref[:, mine]).astype(BF16)
    go(d1[1])
    a1[1, span(first, block), :] = s1[1, span(first, block), :]

    s_a = jnp.floor((s_row + 0.5) * (1.0 / block))
    s_b = s_exp - s_a * n
    swapped = s_b * block + s_a * cap + s_rank
    lane = lax.broadcasted_iota(jnp.int32, (total, total), 1).astype(F32)
    perm[...] = jnp.where(lane == swapped, 1.0, 0.0).astype(BF16)
    last = s_row + core_f * (swapped - s_row)
    fin[...] = jnp.where(lane == last, 1.0, 0.0).astype(BF16)
    back_home, _ = select(e_row)
    pcomb[...] = jnp.where(back_home, 1.0, 0.0).astype(BF16)

    def stage_two(i):
        for copy in d1[i]:
            copy.wait_recv()
        s2[i] = dot(perm[...], a1[i]).astype(BF16)
        go(d2[i])
        a2[i, span(second, block), :] = s2[i, span(second, block), :]

    swap = [
        pltpu.make_async_remote_copy(
            src_ref=rows.at[i, :, mine],
            dst_ref=rows.at[i, :, mine],
            send_sem=cxs.at[i],
            recv_sem=cxr.at[i],
            device_id=other,
            device_id_type=MESH,
        )
        for i in range(2)
    ]

    def stage_three(i):
        for copy in d2[i]:
            copy.wait_recv()
        rows[i, :, mine] = dot(fin[...], a2[i]).astype(BF16)
        go([swap[i]])
        swap[i].wait_recv()

    tile = 256 if hid % 256 == 0 else hid

    def partial(j):
        loads[j].wait()

        def step(f, _):
            cols = span(f, tile)
            if j == 2:
                own[j, :, cols] = dot(rows[1], wd[cols, :], ((1,), (1,)))
            else:
                own[j, :, cols] = dot(rows[0], (wg, wu)[j][:, cols])
            return 0

        lax.fori_loop(0, hid // tile, step, 0)

    def cut(d):
        return slice(0, hh) if d == 0 else slice(hh, hid)

    def rs_copy(d, s, j):
        if s == 0:
            src, dst = st0.at[j, :, cut(d)], rs.at[d, 0, j, :, cut(d)]
        else:
            src, dst = rs.at[d, s - 1, j], rs.at[d, s, j]
        return pltpu.make_async_remote_copy(
            src_ref=src, dst_ref=dst, send_sem=rss.at[d, s, j], recv_sem=rsr.at[d, s, j],
            device_id=z_to[d], device_id_type=MESH,
        )

    ring = {(d, s, j): rs_copy(d, s, j) for d in range(2) for s in range(half_z) for j in range(3)}

    def rs_step(s, j):
        if s == 0:
            st0[j] = own[j, span(z_off(half_z), chunk), :].astype(BF16)
            go([ring[0, 0, j], ring[1, 0, j]])
            return
        for d in range(2):
            sign = 1 - 2 * d
            ring[d, s - 1, j].wait_recv()
            at = span(z_off(sign * (half_z - s)), chunk)
            if s == 1:
                a, b = cut(d), cut(1 - d)
                rs[d, 0, j, :, a] = (rs[d, 0, j, :, a].astype(F32) + own[j, at, a]).astype(BF16)
                rs[d, 0, j, :, b] = own[j, at, b].astype(BF16)
            else:
                rs[d, s - 1, j] = (rs[d, s - 1, j].astype(F32) + own[j, at, :]).astype(BF16)
            go([ring[d, s, j]])

    def rs_sum(j):
        ring[0, half_z - 1, j].wait_recv()
        ring[1, half_z - 1, j].wait_recv()
        return (
            own[j, span(z, chunk), :]
            + rs[0, half_z - 1, j].astype(F32)
            + rs[1, half_z - 1, j].astype(F32)
        )

    def ag_copy(d, s, j):
        at = span(z_off((2 * d - 1) * s), chunk)
        ref = gat.at[j, at, cut(d)] if s == half_z - 1 else gat.at[j, at, :]
        return pltpu.make_async_remote_copy(
            src_ref=ref, dst_ref=ref, send_sem=ags.at[d, s, j], recv_sem=agr.at[d, s, j],
            device_id=z_to[d], device_id_type=MESH,
        )

    def ag_arrived(d, s, j):
        at = span(z_off((2 * d - 1) * (s + 1)), chunk)
        ref = gat.at[j, at, cut(d)] if s == half_z - 1 else gat.at[j, at, :]
        pltpu.make_async_remote_copy(
            src_ref=ref, dst_ref=ref, send_sem=ags.at[d, s, j], recv_sem=agr.at[d, s, j],
            device_id=z_to[d], device_id_type=MESH,
        ).wait_recv()

    stage_two(0)
    stage_two(1)
    stage_three(0)
    partial(0)
    rs_step(0, 0)
    partial(1)
    rs_step(0, 1)
    rs_step(1, 0)
    rs_step(1, 1)
    stage_three(1)
    partial(2)
    rs_step(0, 2)
    for s in range(2, half_z):
        rs_step(s, 0)
        rs_step(s, 1)
        rs_step(s - 1, 2)
    rs_step(half_z - 1, 2)

    here = span(z, chunk)
    gate = rs_sum(0)
    sig = jax.nn.sigmoid(gate)
    silu = gate * sig
    up = rs_sum(1)
    gat[2, here, :] = (silu * up).astype(BF16)
    go([ag_copy(d, 0, 2) for d in range(2)])
    back = rs_sum(2)
    gat[0, here, :] = (back * up * sig * (1.0 + gate * (1.0 - sig))).astype(BF16)
    go([ag_copy(d, 0, 0) for d in range(2)])
    gat[1, here, :] = (back * silu).astype(BF16)
    go([ag_copy(d, 0, 1) for d in range(2)])

    def px_copy(k):
        return pltpu.make_async_remote_copy(
            src_ref=pxo.at[k], dst_ref=pxi.at[k], send_sem=pxs.at[k], recv_sem=pxr.at[k],
            device_id=other, device_id_type=MESH,
        )

    def grads(k):
        at = span(z_off(k), chunk)
        val = dot(gat[0, at, :], wg[...], ((1,), (1,))) + dot(gat[1, at, :], wu[...], ((1,), (1,)))
        keep[k] = val
        pxo[k] = keep[k, :, theirs].astype(BF16)
        go([px_copy(k)])

    def home_copy(k):
        at = z_off(k)
        peer = at // per
        sub = lax.rem(at, per)
        slot = lax.rem(peer + n - my, n) * per + sub
        return pltpu.make_async_remote_copy(
            src_ref=rt.at[k], dst_ref=ra.at[span(my * per + sub, chunk), :],
            send_sem=r1s.at[slot], recv_sem=r1r.at[slot],
            device_id=at_y(peer), device_id_type=MESH,
        )

    def settle(k):
        px_copy(k).wait_recv()
        val = (keep[k, :, mine] + pxi[k].astype(F32)).astype(BF16)
        rt[k] = val
        at = z_off(k)

        @pl.when(at // per == my)
        def _():
            ra[span(at, chunk), :] = val

        @pl.when(at // per != my)
        def _():
            home_copy(k).start()

    grads(0)
    done = [0]
    for s in range(1, half_z + 1):
        for j in (2, 0, 1):
            for d in range(2):
                ag_arrived(d, s - 1, j)
                if s < half_z:
                    go([ag_copy(d, s, j)])
        for k in done:
            settle(k)
        done = [s, nz - s] if s < half_z else [s]
        if s == half_z:
            grads(s)
        else:
            grads(s)
            grads(nz - s)
    ftile = 256 if hid % 256 == 0 else hid

    def down(f, _):
        cols = span(f, ftile)
        dgrad_ref[cols, :] = dot(gat[2, :, cols], rows[1], ((0,), (0,))).astype(BF16)
        return 0

    for k in done:
        settle(k)
    lax.fori_loop(0, hid // ftile, down, 0)

    for r in range(1, n):
        for sub in range(per):
            slot = r * per + sub
            pltpu.make_async_remote_copy(
                src_ref=rt.at[0],
                dst_ref=ra.at[span(lax.rem(my + n - r, n) * per + sub, chunk), :],
                send_sem=r1s.at[slot], recv_sem=r1r.at[slot],
                device_id=at_y(lax.rem(my + r, n)), device_id_type=MESH,
            ).wait_recv()
    r2[...] = dot(perm[...], ra[...]).astype(BF16)
    home = exchange(r2, rc, r2s, r2r, mx, at_x)
    go(home)
    rc[span(mx, block), :] = r2[span(mx, block), :]
    for copy in home:
        copy.wait_recv()
    res[:, mine] = dot(pcomb[...], rc[...], ((0,), (0,))).astype(BF16)
    last_swap = pltpu.make_async_remote_copy(
        src_ref=res.at[:, mine], dst_ref=res.at[:, mine], send_sem=fs.at[0], recv_sem=fr.at[0],
        device_id=other, device_id_type=MESH,
    )
    go([last_swap])
    last_swap.wait_recv()
    dx_ref[...] = res[...]

    for copy in pending:
        copy.wait_send()
    for k in range(nz):
        at = z_off(k)

        @pl.when(at // per != my)
        def _():
            home_copy(k).wait_send()


def body(tokens, cotangent, routes, gates, w_gate, w_up, w_down):
    tok, width = tokens.shape
    top = routes.shape[1]
    hid = w_gate.shape[2]
    experts = lax.axis_size("expert")
    nz = lax.axis_size("dp")
    n = math.isqrt(experts)
    cap = max(2, 5 * tok * top // (4 * experts))
    total = experts * cap
    chunk = total // nz
    hw = width // 2
    hz = nz // 2
    vm = pltpu.VMEM
    dma = pltpu.SemaphoreType.DMA
    in_vmem = pl.BlockSpec(memory_space=pltpu.VMEM)
    in_hbm = pl.BlockSpec(memory_space=pl.ANY)
    scratch = [
        vm((width, hid), BF16), vm((width, hid), BF16), vm((hid, width), BF16),
        vm((total, total), BF16), vm((total, total), BF16), vm((total, tok), BF16),
        vm((2, total, hw), BF16), vm((2, total, hw), BF16), vm((2, total, hw), BF16), vm((2, total, hw), BF16),
        vm((2, total, width), BF16),
        vm((3, total, hid), F32),
        vm((3, chunk, hid), BF16),
        vm((2, hz, 3, chunk, hid), BF16),
        vm((3, total, hid), BF16),
        vm((nz, chunk, width), F32),
        vm((nz, chunk, hw), BF16), vm((nz, chunk, hw), BF16), vm((nz, chunk, hw), BF16),
        vm((total, hw), BF16), vm((total, hw), BF16), vm((total, hw), BF16),
        vm((tok, width), BF16),
        dma((3,)),
        dma((2, n)), dma((2, n)), dma((2, n)), dma((2, n)),
        dma((2,)), dma((2,)),
        dma((2, hz, 3)), dma((2, hz, 3)), dma((2, hz, 3)), dma((2, hz, 3)),
        dma((nz,)), dma((nz,)),
        dma((nz,)), dma((nz,)),
        dma((n,)), dma((n,)),
        dma((1,)), dma((1,)),
    ]
    dx, dgrad = pl.pallas_call(
        functools.partial(kernel, (n, nz, cap, tok, top, width, hid)),
        out_shape=(
            jax.ShapeDtypeStruct((tok, width), BF16),
            jax.ShapeDtypeStruct((hid, width), BF16),
        ),
        in_specs=[in_vmem] * 4 + [in_hbm] * 3,
        out_specs=(in_vmem, in_vmem),
        scratch_shapes=scratch,
        compiler_params=pltpu.CompilerParams(
            collective_id=0, has_side_effects=True, vmem_limit_bytes=52 * 1024 * 1024
        ),
        cost_estimate=pl.CostEstimate(
            flops=12 * total * width * hid, bytes_accessed=8 * width * hid, transcendentals=chunk * hid
        ),
    )(routes.T, gates.T, tokens, cotangent, w_gate[0], w_up[0], w_down[0])
    return dx, dgrad[None]


def solution(mesh):
    return jax.shard_map(
        body,
        mesh=mesh,
        in_specs=(
            P("expert", "dp"),
            P("expert", "dp"),
            P("expert", None),
            P("expert", None),
            P("expert", "dp", "tensor"),
            P("expert", "dp", "tensor"),
            P("expert", "tensor", "dp"),
        ),
        out_specs=(P("expert", "dp"), P("expert", "tensor", "dp")),
        check_vma=False,
    )
```

```python
import functools
import math

import jax
import jax.numpy as jnp
from jax import lax
from jax.experimental import pallas as pl
from jax.experimental.pallas import tpu as pltpu
from jax.sharding import PartitionSpec as P

MESH = pl.DeviceIdType.MESH
F32 = jnp.float32
BF16 = jnp.bfloat16


def dot(a, b, dims=((1,), (0,))):
    return lax.dot_general(a, b, (dims, ((), ())), preferred_element_type=F32)


def kernel(
    c,
    routes_hbm, gates_hbm, tok_hbm, cot_hbm, wg_hbm, wu_hbm, wd_hbm,
    dx_ref, dgrad_ref,
    routes_ref, gates_ref, tok_ref, cot_ref, wg, wu, wd, perm, fin, pcomb, pad,
    s1, a1, s2, a2, rows, own, st0, rs, gat, keep, pxo, pxi, rt, rc, res,
    wsem, d1s, d1r, d2s, d2r, cxs, cxr, rss, rsr, ags, agr, pxs, pxr, hs, hr, fs, fr,
):
    n, nz, cap, tok, top, width, hid = c
    half_z = nz // 2
    total = n * n * cap
    chunk = total // nz
    block = n * cap
    pieces = n * n // nz
    room = -(-cap // 16) * 16
    hw = width // 2
    hh = hid // 2
    order = [r for pair in zip(range(n // 2, 0, -1), range(n - n // 2, n)) for r in pair]
    order = list(dict.fromkeys(r for r in order if 0 < r < n))

    z = lax.axis_index("dp")
    core = lax.axis_index("tensor")
    me = lax.axis_index("expert")
    mx, my = me // n, lax.rem(me, n)
    first = (1 - core) * mx + core * my
    second = (1 - core) * my + core * mx

    def at_first(p):
        return {"expert": (1 - core) * (p * n + my) + core * (mx * n + p)}

    def at_second(p):
        return {"expert": (1 - core) * (mx * n + p) + core * (p * n + my)}

    other = {"tensor": 1 - core}
    z_to = ({"dp": lax.rem(z + 1, nz)}, {"dp": lax.rem(z + nz - 1, nz)})

    def z_off(k):
        return lax.rem(z + k + 2 * nz, nz)

    def span(i, size):
        return pl.ds(pl.multiple_of(i * size, size), size)

    mine = span(core, hw)
    theirs = span(1 - core, hw)

    inputs = [
        pltpu.make_async_copy(src, dst, wsem.at[i])
        for i, (src, dst) in enumerate((
            (routes_hbm, routes_ref), (gates_hbm, gates_ref), (tok_hbm, tok_ref), (cot_hbm, cot_ref),
            (wg_hbm, wg), (wu_hbm, wu), (wd_hbm, wd),
        ))
    ]
    for load in inputs:
        load.start()
    loads = inputs[4:]

    ex = n * n
    barrier = pltpu.get_barrier_semaphore()

    def greet(r, _):
        pl.semaphore_signal(barrier, inc=1, device_id={"expert": lax.rem(me + r, ex)}, device_id_type=MESH)
        return 0

    lax.fori_loop(1, ex, greet, 0)
    for peer in (other, z_to[0], z_to[1]):
        pl.semaphore_signal(barrier, inc=1, device_id=peer, device_id_type=MESH)

    e_row = lax.broadcasted_iota(jnp.int32, (ex, 1), 0).astype(F32)
    e_div = jnp.floor((e_row + 0.5) * (1.0 / n))
    e_swap = (e_row - e_div * n) * n + e_div
    core_f = core.astype(F32)
    e_disp = e_row + core_f * (e_swap - e_row)
    s_row = lax.broadcasted_iota(jnp.int32, (total, 1), 0).astype(F32)
    s_exp = jnp.floor((s_row + 0.5) * (1.0 / cap))
    s_rank = s_row - s_exp * cap
    expand = (s_exp == lax.broadcasted_iota(jnp.int32, (total, ex), 1).astype(F32)).astype(BF16)
    earlier = (
        lax.broadcasted_iota(jnp.int32, (tok, tok), 0) < lax.broadcasted_iota(jnp.int32, (tok, tok), 1)
    ).astype(BF16)
    inputs[0].wait()
    inputs[1].wait()
    routes = routes_ref[...].astype(F32)
    gates = gates_ref[...].astype(F32)

    def select(names):
        member = jnp.zeros((ex, tok), F32)
        weight = jnp.zeros((ex, tok), F32)
        for k in range(top):
            hit = routes[k : k + 1, :] == names
            member = member + jnp.where(hit, 1.0, 0.0)
            weight = weight + jnp.where(hit, gates[k : k + 1, :], 0.0)
        rank = dot(member.astype(BF16), earlier)
        placed = (member * (rank + 1.0)).astype(BF16)
        return placed, weight

    placed, weight = select(e_disp)
    picked = dot(expand, placed) == s_rank + 1.0
    chosen = jnp.where(picked, 1.0, 0.0).astype(BF16)
    inputs[2].wait()
    s1[0] = dot(chosen, tok_ref[:, mine]).astype(BF16)

    pl.semaphore_wait(barrier, ex + 2)

    def exchange(src, dst, ssem, rsem, here, where):
        out = []
        for r in order:
            peer = lax.rem(here + r, n)
            out.append(
                pltpu.make_async_remote_copy(
                    src_ref=src.at[span(peer, block), :],
                    dst_ref=dst.at[span(here, block), :],
                    send_sem=ssem.at[r],
                    recv_sem=rsem.at[r],
                    device_id=where(peer),
                    device_id_type=MESH,
                )
            )
        return out

    pending = []

    def go(copies):
        for copy in copies:
            copy.start()
            pending.append(copy)

    d1 = [exchange(s1.at[i], a1.at[i], d1s.at[i], d1r.at[i], first, at_first) for i in range(2)]
    d2 = [exchange(s2.at[i], a2.at[i], d2s.at[i], d2r.at[i], second, at_second) for i in range(2)]

    go(d1[0])
    a1[0, span(first, block), :] = s1[0, span(first, block), :]

    s_a = jnp.floor((s_row + 0.5) * (1.0 / block))
    s_b = s_exp - s_a * n
    lane = lax.broadcasted_iota(jnp.int32, (total, total), 1).astype(F32)
    perm[...] = jnp.where(lane == s_b * block + s_a * cap + s_rank, 1.0, 0.0).astype(BF16)

    weighted = jnp.where(picked, dot(expand, weight.astype(BF16)), 0.0).astype(BF16)
    inputs[3].wait()
    s1[1] = dot(weighted, cot_ref[:, mine]).astype(BF16)
    go(d1[1])
    a1[1, span(first, block), :] = s1[1, span(first, block), :]

    def stage_two(i):
        for copy in d1[i]:
            copy.wait_recv()
        s2[i] = dot(perm[...], a1[i]).astype(BF16)
        go(d2[i])
        a2[i, span(second, block), :] = s2[i, span(second, block), :]

    swap = [
        pltpu.make_async_remote_copy(
            src_ref=rows.at[i, :, mine],
            dst_ref=rows.at[i, :, mine],
            send_sem=cxs.at[i],
            recv_sem=cxr.at[i],
            device_id=other,
            device_id_type=MESH,
        )
        for i in range(2)
    ]

    def stage_three(i):
        if i:
            for copy in d2[i]:
                copy.wait_recv()
        rows[i, :, mine] = dot(fin[...], a2[i]).astype(BF16)
        go([swap[i]])
        swap[i].wait_recv()

    tile = 256 if hid % 256 == 0 else hid

    def partial(j):
        loads[j].wait()

        def step(f, _):
            cols = span(f, tile)
            if j == 2:
                own[j, :, cols] = dot(rows[1], wd[cols, :], ((1,), (1,)))
            else:
                own[j, :, cols] = dot(rows[0], (wg, wu)[j][:, cols])
            return 0

        lax.fori_loop(0, hid // tile, step, 0)

    def cut(d):
        return slice(0, hh) if d == 0 else slice(hh, hid)

    def rs_copy(d, s, j):
        if s == 0:
            src, dst = st0.at[j, :, cut(d)], rs.at[d, 0, j, :, cut(d)]
        else:
            src, dst = rs.at[d, s - 1, j], rs.at[d, s, j]
        return pltpu.make_async_remote_copy(
            src_ref=src, dst_ref=dst, send_sem=rss.at[d, s, j], recv_sem=rsr.at[d, s, j],
            device_id=z_to[d], device_id_type=MESH,
        )

    ring = {(d, s, j): rs_copy(d, s, j) for d in range(2) for s in range(half_z) for j in range(3)}

    def rs_step(s, j):
        if s == 0:
            st0[j] = own[j, span(z_off(half_z), chunk), :].astype(BF16)
            go([ring[0, 0, j], ring[1, 0, j]])
            return
        for d in range(2):
            sign = 1 - 2 * d
            ring[d, s - 1, j].wait_recv()
            at = span(z_off(sign * (half_z - s)), chunk)
            if s == 1:
                a, b = cut(d), cut(1 - d)
                rs[d, 0, j, :, a] = (rs[d, 0, j, :, a].astype(F32) + own[j, at, a]).astype(BF16)
                rs[d, 0, j, :, b] = own[j, at, b].astype(BF16)
            else:
                rs[d, s - 1, j] = (rs[d, s - 1, j].astype(F32) + own[j, at, :]).astype(BF16)
            go([ring[d, s, j]])

    def rs_sum(j):
        ring[0, half_z - 1, j].wait_recv()
        ring[1, half_z - 1, j].wait_recv()
        return (
            own[j, span(z, chunk), :]
            + rs[0, half_z - 1, j].astype(F32)
            + rs[1, half_z - 1, j].astype(F32)
        )

    def ag_copy(d, s, j):
        at = span(z_off((2 * d - 1) * s), chunk)
        ref = gat.at[j, at, cut(d)] if s == half_z - 1 else gat.at[j, at, :]
        return pltpu.make_async_remote_copy(
            src_ref=ref, dst_ref=ref, send_sem=ags.at[d, s, j], recv_sem=agr.at[d, s, j],
            device_id=z_to[d], device_id_type=MESH,
        )

    def ag_arrived(d, s, j):
        at = span(z_off((2 * d - 1) * (s + 1)), chunk)
        ref = gat.at[j, at, cut(d)] if s == half_z - 1 else gat.at[j, at, :]
        pltpu.make_async_remote_copy(
            src_ref=ref, dst_ref=ref, send_sem=ags.at[d, s, j], recv_sem=agr.at[d, s, j],
            device_id=z_to[d], device_id_type=MESH,
        ).wait_recv()

    stage_two(0)
    stage_two(1)
    s_d = jnp.floor((s_exp + 0.5) * (1.0 / pieces))
    s_x = jnp.floor((s_d + 0.5) * (1.0 / n)) * pieces + (s_exp - s_d * pieces)
    s_y = s_d + s_x + (mx + my).astype(F32)
    s_y = s_y - jnp.floor((s_y + 0.5) * (1.0 / n)) * n
    by_y = s_y * block + s_x * cap + s_rank
    by_x = s_x * block + s_y * cap + s_rank
    fin[...] = jnp.where(lane == by_y + core_f * (by_x - by_y), 1.0, 0.0).astype(BF16)
    for copy in d2[0]:
        copy.wait_recv()
    stage_three(0)
    partial(0)
    rs_step(0, 0)
    partial(1)
    rs_step(0, 1)
    rs_step(1, 0)
    rs_step(1, 1)
    stage_three(1)
    partial(2)
    rs_step(0, 2)
    for s in range(2, half_z):
        rs_step(s, 0)
        rs_step(s, 1)
        rs_step(s - 1, 2)

    here = span(z, chunk)
    gate = rs_sum(0)
    sig = jax.nn.sigmoid(gate)
    silu = gate * sig
    up = rs_sum(1)
    gat[2, here, :] = (silu * up).astype(BF16)
    go([ag_copy(d, 0, 2) for d in range(2)])
    rs_step(half_z - 1, 2)
    back = rs_sum(2)
    gat[0, here, :] = (back * up * sig * (1.0 + gate * (1.0 - sig))).astype(BF16)
    go([ag_copy(d, 0, 0) for d in range(2)])
    gat[1, here, :] = (back * silu).astype(BF16)
    go([ag_copy(d, 0, 1) for d in range(2)])

    def px_copy(k):
        return pltpu.make_async_remote_copy(
            src_ref=pxo.at[k], dst_ref=pxi.at[k], send_sem=pxs.at[k], recv_sem=pxr.at[k],
            device_id=other, device_id_type=MESH,
        )

    def grads(k):
        at = span(z_off(k), chunk)
        val = dot(gat[0, at, :], wg[...], ((1,), (1,))) + dot(gat[1, at, :], wu[...], ((1,), (1,)))
        keep[k] = val
        pxo[k] = keep[k, :, theirs].astype(BF16)
        go([px_copy(k)])

    def piece(k, p):
        at = z_off(k)
        px = (at // n * pieces if nz > n else 0) + p
        peer = px * n + lax.rem(at + px + mx + my, n)
        return peer, pltpu.make_async_remote_copy(
            src_ref=rt.at[k, span(p, room), :], dst_ref=rc.at[span(me, room), :],
            send_sem=hs.at[k * pieces + p], recv_sem=hr.at[me],
            device_id={"expert": peer}, device_id_type=MESH,
        )

    def settle(k):
        px_copy(k).wait_recv()
        val = (keep[k, :, mine] + pxi[k].astype(F32)).astype(BF16)
        rt[k] = dot(pad[...], val).astype(BF16)

        def send(p, _):
            peer, copy = piece(k, p)

            @pl.when(peer != me)
            def _():
                copy.start()

            @pl.when(peer == me)
            def _():
                rc[span(me, room), :] = rt[k, span(p, room), :]

            return 0

        lax.fori_loop(0, pieces, send, 0)

    grads(0)

    p_row = lax.broadcasted_iota(jnp.int32, (pieces * room, 1), 0).astype(F32)
    p_div = jnp.floor((p_row + 0.5) * (1.0 / room))
    p_rank = p_row - p_div * room
    p_lane = lax.broadcasted_iota(jnp.int32, (pieces * room, chunk), 1).astype(F32)
    pad[...] = jnp.where((p_lane == p_div * cap + p_rank) & (p_rank < cap), 1.0, 0.0).astype(BF16)
    h_row = lax.broadcasted_iota(jnp.int32, (ex * room, 1), 0).astype(F32)
    h_exp = jnp.floor((h_row + 0.5) * (1.0 / room))
    h_rank = h_row - h_exp * room
    unfold = (h_exp == lax.broadcasted_iota(jnp.int32, (ex * room, ex), 1).astype(F32)).astype(BF16)
    placed, _ = select(e_row)
    h_hit = (dot(unfold, placed) == h_rank + 1.0) & (h_rank < cap)
    eye = (
        lax.broadcasted_iota(jnp.int32, (tok, tok), 0) == lax.broadcasted_iota(jnp.int32, (tok, tok), 1)
    ).astype(BF16)
    pcomb[...] = dot(eye, jnp.where(h_hit, 1.0, 0.0).astype(BF16), ((1,), (1,))).astype(BF16)

    def forward(s, j):
        for d in range(2):
            ag_arrived(d, s - 1, j)
            if s < half_z:
                go([ag_copy(d, s, j)])

    done = [0]
    for s in range(1, half_z):
        forward(s, 0)
        settle(done[0])
        forward(s, 1)
        grads(s)
        if len(done) > 1:
            settle(done[1])
        forward(s, 2)
        grads(nz - s)
        done = [s, nz - s]
    for k in done:
        settle(k)
    forward(half_z, 0)
    forward(half_z, 1)
    grads(half_z)
    settle(half_z)

    for d in range(2):
        ag_arrived(d, half_z - 1, 2)
    ftile = 256 if hid % 256 == 0 else hid

    def down(f, _):
        cols = span(f, ftile)
        dgrad_ref[cols, :] = dot(gat[2, :, cols], rows[1], ((0,), (0,))).astype(BF16)
        return 0

    lax.fori_loop(0, hid // ftile, down, 0)

    for copy in pending:
        copy.wait_send()

    def sent(i, _):
        k, p = i // pieces, lax.rem(i, pieces)
        peer, copy = piece(k, p)

        @pl.when(peer != me)
        def _():
            copy.wait_send()

        return 0

    lax.fori_loop(0, ex, sent, 0)

    def arrive(e, _):
        @pl.when(e != me)
        def _():
            pltpu.make_async_remote_copy(
                src_ref=rt.at[0, span(0, room), :], dst_ref=rc.at[span(e, room), :],
                send_sem=hs.at[0], recv_sem=hr.at[e],
                device_id={"expert": e}, device_id_type=MESH,
            ).wait_recv()

        return 0

    lax.fori_loop(0, ex, arrive, 0)
    res[:, mine] = dot(pcomb[...], rc[...]).astype(BF16)
    last_swap = pltpu.make_async_remote_copy(
        src_ref=res.at[:, mine], dst_ref=res.at[:, mine], send_sem=fs.at[0], recv_sem=fr.at[0],
        device_id=other, device_id_type=MESH,
    )
    last_swap.start()
    last_swap.wait_recv()
    dx_ref[...] = res[...]

    last_swap.wait_send()


def body(tokens, cotangent, routes, gates, w_gate, w_up, w_down):
    tok, width = tokens.shape
    top = routes.shape[1]
    hid = w_gate.shape[2]
    experts = lax.axis_size("expert")
    nz = lax.axis_size("dp")
    n = math.isqrt(experts)
    cap = max(2, 5 * tok * top // (4 * experts))
    total = experts * cap
    chunk = total // nz
    hw = width // 2
    hz = nz // 2
    pieces = experts // nz
    room = -(-cap // 16) * 16
    vm = pltpu.VMEM
    dma = pltpu.SemaphoreType.DMA
    in_vmem = pl.BlockSpec(memory_space=pltpu.VMEM)
    in_hbm = pl.BlockSpec(memory_space=pltpu.HBM)
    scratch = [
        vm((top, tok), routes.dtype), vm((top, tok), BF16), vm((tok, width), BF16), vm((tok, width), BF16),
        vm((width, hid), BF16), vm((width, hid), BF16), vm((hid, width), BF16),
        vm((total, total), BF16), vm((total, total), BF16), vm((tok, experts * room), BF16),
        vm((pieces * room, chunk), BF16),
        vm((2, total, hw), BF16), vm((2, total, hw), BF16), vm((2, total, hw), BF16), vm((2, total, hw), BF16),
        vm((2, total, width), BF16),
        vm((3, total, hid), F32),
        vm((3, chunk, hid), BF16),
        vm((2, hz, 3, chunk, hid), BF16),
        vm((3, total, hid), BF16),
        vm((nz, chunk, width), F32),
        vm((nz, chunk, hw), BF16), vm((nz, chunk, hw), BF16),
        vm((nz, pieces * room, hw), BF16), vm((experts * room, hw), BF16),
        vm((tok, width), BF16),
        dma((7,)),
        dma((2, n)), dma((2, n)), dma((2, n)), dma((2, n)),
        dma((2,)), dma((2,)),
        dma((2, hz, 3)), dma((2, hz, 3)), dma((2, hz, 3)), dma((2, hz, 3)),
        dma((nz,)), dma((nz,)),
        dma((experts,)), dma((experts,)),
        dma((1,)), dma((1,)),
    ]
    dx, dgrad = pl.pallas_call(
        functools.partial(kernel, (n, nz, cap, tok, top, width, hid)),
        out_shape=(
            jax.ShapeDtypeStruct((tok, width), BF16),
            jax.ShapeDtypeStruct((hid, width), BF16),
        ),
        in_specs=[in_hbm] * 7,
        out_specs=(in_vmem, in_vmem),
        scratch_shapes=scratch,
        compiler_params=pltpu.CompilerParams(
            collective_id=0, has_side_effects=True, vmem_limit_bytes=62 * 1024 * 1024
        ),
        cost_estimate=pl.CostEstimate(
            flops=12 * total * width * hid, bytes_accessed=8 * width * hid, transcendentals=chunk * hid
        ),
    )(routes.T, gates.T, tokens, cotangent, w_gate[0], w_up[0], w_down[0])
    return dx, dgrad[None]


def solution(mesh):
    return jax.shard_map(
        body,
        mesh=mesh,
        in_specs=(
            P("expert", "dp"),
            P("expert", "dp"),
            P("expert", None),
            P("expert", None),
            P("expert", "dp", "tensor"),
            P("expert", "dp", "tensor"),
            P("expert", "tensor", "dp"),
        ),
        out_specs=(P("expert", "dp"), P("expert", "tensor", "dp")),
        check_vma=False,
    )
```

```python
import functools
import math

import jax
import jax.numpy as jnp
from jax import lax
from jax.experimental import pallas as pl
from jax.experimental.pallas import tpu as pltpu
from jax.sharding import PartitionSpec as P

MESH = pl.DeviceIdType.MESH
F32 = jnp.float32
BF16 = jnp.bfloat16


def dot(a, b, dims=((1,), (0,))):
    return lax.dot_general(a, b, (dims, ((), ())), preferred_element_type=F32)


def kernel(
    c,
    routes_hbm, gates_hbm, tok_hbm, cot_hbm, wg_hbm, wu_hbm, wd_hbm,
    dx_hbm, dgrad_hbm,
    dgrad_ref, routes_ref, gates_ref, tok_ref, cot_ref, wg, wu, wd, perm, fin, pcomb, pad,
    s1, a1, s2, a2, rows, own, st0, rs, gat, keep, pxo, pxi, rt, rc, res,
    wsem, d1s, d1r, d2s, d2r, cxs, cxr, rss, rsr, ags, agr, pxs, pxr, hs, hr, fs, fr,
):
    n, nz, cap, tok, top, width, hid = c
    half_z = nz // 2
    total = n * n * cap
    chunk = total // nz
    block = n * cap
    pieces = n * n // nz
    room = -(-cap // 16) * 16
    hw = width // 2
    hh = hid // 2
    order = [r for pair in zip(range(n // 2, 0, -1), range(n - n // 2, n)) for r in pair]
    order = list(dict.fromkeys(r for r in order if 0 < r < n))

    z = lax.axis_index("dp")
    core = lax.axis_index("tensor")
    me = lax.axis_index("expert")
    mx, my = me // n, lax.rem(me, n)
    first = (1 - core) * mx + core * my
    second = (1 - core) * my + core * mx

    def at_first(p):
        return {"expert": (1 - core) * (p * n + my) + core * (mx * n + p)}

    def at_second(p):
        return {"expert": (1 - core) * (mx * n + p) + core * (p * n + my)}

    other = {"tensor": 1 - core}
    z_to = ({"dp": lax.rem(z + 1, nz)}, {"dp": lax.rem(z + nz - 1, nz)})

    def z_off(k):
        return lax.rem(z + k + 2 * nz, nz)

    def span(i, size):
        return pl.ds(pl.multiple_of(i * size, size), size)

    mine = span(core, hw)
    theirs = span(1 - core, hw)

    inputs = [
        pltpu.make_async_copy(src, dst, wsem.at[i])
        for i, (src, dst) in enumerate((
            (routes_hbm, routes_ref), (gates_hbm, gates_ref), (tok_hbm, tok_ref), (cot_hbm, cot_ref),
            (wg_hbm, wg), (wu_hbm, wu), (wd_hbm, wd),
        ))
    ]
    for load in inputs:
        load.start()
    loads = inputs[4:]

    ex = n * n
    barrier = pltpu.get_barrier_semaphore()

    def greet(r, _):
        pl.semaphore_signal(barrier, inc=1, device_id={"expert": lax.rem(me + r, ex)}, device_id_type=MESH)
        return 0

    lax.fori_loop(1, ex, greet, 0)
    for peer in (other, z_to[0], z_to[1]):
        pl.semaphore_signal(barrier, inc=1, device_id=peer, device_id_type=MESH)

    e_row = lax.broadcasted_iota(jnp.int32, (ex, 1), 0).astype(F32)
    e_div = jnp.floor((e_row + 0.5) * (1.0 / n))
    e_swap = (e_row - e_div * n) * n + e_div
    core_f = core.astype(F32)
    e_disp = e_row + core_f * (e_swap - e_row)
    s_row = lax.broadcasted_iota(jnp.int32, (total, 1), 0).astype(F32)
    s_exp = jnp.floor((s_row + 0.5) * (1.0 / cap))
    s_rank = s_row - s_exp * cap
    expand = (s_exp == lax.broadcasted_iota(jnp.int32, (total, ex), 1).astype(F32)).astype(BF16)
    earlier = (
        lax.broadcasted_iota(jnp.int32, (tok, tok), 0) < lax.broadcasted_iota(jnp.int32, (tok, tok), 1)
    ).astype(BF16)
    inputs[0].wait()
    inputs[1].wait()
    routes = routes_ref[...].astype(F32)
    gates = gates_ref[...].astype(F32)

    def select(names):
        member = jnp.zeros((ex, tok), F32)
        weight = jnp.zeros((ex, tok), F32)
        for k in range(top):
            hit = routes[k : k + 1, :] == names
            member = member + jnp.where(hit, 1.0, 0.0)
            weight = weight + jnp.where(hit, gates[k : k + 1, :], 0.0)
        rank = dot(member.astype(BF16), earlier)
        placed = (member * (rank + 1.0)).astype(BF16)
        return placed, weight

    placed, weight = select(e_disp)
    picked = dot(expand, placed) == s_rank + 1.0
    chosen = jnp.where(picked, 1.0, 0.0).astype(BF16)
    inputs[2].wait()
    s1[0] = dot(chosen, tok_ref[:, mine]).astype(BF16)

    pl.semaphore_wait(barrier, ex + 2)

    def exchange(src, dst, ssem, rsem, here, where):
        out = []
        for r in order:
            peer = lax.rem(here + r, n)
            out.append(
                pltpu.make_async_remote_copy(
                    src_ref=src.at[span(peer, block), :],
                    dst_ref=dst.at[span(here, block), :],
                    send_sem=ssem.at[r],
                    recv_sem=rsem.at[r],
                    device_id=where(peer),
                    device_id_type=MESH,
                )
            )
        return out

    pending = []

    def go(copies):
        for copy in copies:
            copy.start()
            pending.append(copy)

    d1 = [exchange(s1.at[i], a1.at[i], d1s.at[i], d1r.at[i], first, at_first) for i in range(2)]
    d2 = [exchange(s2.at[i], a2.at[i], d2s.at[i], d2r.at[i], second, at_second) for i in range(2)]

    go(d1[0])
    a1[0, span(first, block), :] = s1[0, span(first, block), :]

    s_a = jnp.floor((s_row + 0.5) * (1.0 / block))
    s_b = s_exp - s_a * n
    lane = lax.broadcasted_iota(jnp.int32, (total, total), 1).astype(F32)
    perm[...] = jnp.where(lane == s_b * block + s_a * cap + s_rank, 1.0, 0.0).astype(BF16)

    weighted = jnp.where(picked, dot(expand, weight.astype(BF16)), 0.0).astype(BF16)
    inputs[3].wait()
    s1[1] = dot(weighted, cot_ref[:, mine]).astype(BF16)
    go(d1[1])
    a1[1, span(first, block), :] = s1[1, span(first, block), :]

    def stage_two(i):
        for copy in d1[i]:
            copy.wait_recv()
        s2[i] = dot(perm[...], a1[i]).astype(BF16)
        go(d2[i])
        a2[i, span(second, block), :] = s2[i, span(second, block), :]

    swap = [
        pltpu.make_async_remote_copy(
            src_ref=rows.at[i, :, mine],
            dst_ref=rows.at[i, :, mine],
            send_sem=cxs.at[i],
            recv_sem=cxr.at[i],
            device_id=other,
            device_id_type=MESH,
        )
        for i in range(2)
    ]

    def stage_three(i):
        if i:
            for copy in d2[i]:
                copy.wait_recv()
        rows[i, :, mine] = dot(fin[...], a2[i]).astype(BF16)
        go([swap[i]])
        swap[i].wait_recv()

    tile = 256 if hid % 256 == 0 else hid

    def partial(j):
        def step(f, _):
            cols = span(f, tile)
            if j == 2:
                own[j, :, cols] = dot(rows[1], wd[cols, :], ((1,), (1,)))
            else:
                own[j, :, cols] = dot(rows[0], (wg, wu)[j][:, cols])
            return 0

        lax.fori_loop(0, hid // tile, step, 0)

    def cut(d):
        return slice(0, hh) if d == 0 else slice(hh, hid)

    def rs_copy(d, s, j):
        if s == 0:
            src, dst = st0.at[j, :, cut(d)], rs.at[d, 0, j, :, cut(d)]
        else:
            src, dst = rs.at[d, s - 1, j], rs.at[d, s, j]
        return pltpu.make_async_remote_copy(
            src_ref=src, dst_ref=dst, send_sem=rss.at[d, s, j], recv_sem=rsr.at[d, s, j],
            device_id=z_to[d], device_id_type=MESH,
        )

    ring = {(d, s, j): rs_copy(d, s, j) for d in range(2) for s in range(half_z) for j in range(3)}

    def rs_step(s, j):
        if s == 0:
            far = span(z_off(half_z), chunk)
            loads[j].wait()
            if j == 2:
                st0[j] = dot(rows[1, far, :], wd[...], ((1,), (1,))).astype(BF16)
            else:
                st0[j] = dot(rows[0, far, :], (wg, wu)[j][...]).astype(BF16)
            go([ring[0, 0, j], ring[1, 0, j]])
            return
        for d in range(2):
            sign = 1 - 2 * d
            ring[d, s - 1, j].wait_recv()
            at = span(z_off(sign * (half_z - s)), chunk)
            if s == 1:
                a, b = cut(d), cut(1 - d)
                rs[d, 0, j, :, a] = (rs[d, 0, j, :, a].astype(F32) + own[j, at, a]).astype(BF16)
                rs[d, 0, j, :, b] = own[j, at, b].astype(BF16)
            else:
                rs[d, s - 1, j] = (rs[d, s - 1, j].astype(F32) + own[j, at, :]).astype(BF16)
            go([ring[d, s, j]])

    def rs_sum(j):
        ring[0, half_z - 1, j].wait_recv()
        ring[1, half_z - 1, j].wait_recv()
        return (
            own[j, span(z, chunk), :]
            + rs[0, half_z - 1, j].astype(F32)
            + rs[1, half_z - 1, j].astype(F32)
        )

    def ag_copy(d, s, j):
        at = span(z_off((2 * d - 1) * s), chunk)
        ref = gat.at[j, at, cut(d)] if s == half_z - 1 else gat.at[j, at, :]
        return pltpu.make_async_remote_copy(
            src_ref=ref, dst_ref=ref, send_sem=ags.at[d, s, j], recv_sem=agr.at[d, s, j],
            device_id=z_to[d], device_id_type=MESH,
        )

    def ag_arrived(d, s, j):
        at = span(z_off((2 * d - 1) * (s + 1)), chunk)
        ref = gat.at[j, at, cut(d)] if s == half_z - 1 else gat.at[j, at, :]
        pltpu.make_async_remote_copy(
            src_ref=ref, dst_ref=ref, send_sem=ags.at[d, s, j], recv_sem=agr.at[d, s, j],
            device_id=z_to[d], device_id_type=MESH,
        ).wait_recv()

    stage_two(0)
    stage_two(1)
    s_d = jnp.floor((s_exp + 0.5) * (1.0 / pieces))
    s_x = jnp.floor((s_d + 0.5) * (1.0 / n)) * pieces + (s_exp - s_d * pieces)
    s_y = s_d + s_x + (mx + my).astype(F32)
    s_y = s_y - jnp.floor((s_y + 0.5) * (1.0 / n)) * n
    by_y = s_y * block + s_x * cap + s_rank
    by_x = s_x * block + s_y * cap + s_rank
    fin[...] = jnp.where(lane == by_y + core_f * (by_x - by_y), 1.0, 0.0).astype(BF16)
    for copy in d2[0]:
        copy.wait_recv()
    stage_three(0)
    rs_step(0, 0)
    rs_step(0, 1)
    partial(0)
    partial(1)
    rs_step(1, 0)
    rs_step(1, 1)
    stage_three(1)
    rs_step(0, 2)
    partial(2)
    for s in range(2, half_z):
        rs_step(s, 0)
        rs_step(s, 1)
        rs_step(s - 1, 2)

    here = span(z, chunk)
    gate = rs_sum(0)
    sig = jax.nn.sigmoid(gate)
    silu = gate * sig
    up = rs_sum(1)
    gat[2, here, :] = (silu * up).astype(BF16)
    go([ag_copy(d, 0, 2) for d in range(2)])
    rs_step(half_z - 1, 2)
    back = rs_sum(2)
    gat[0, here, :] = (back * up * sig * (1.0 + gate * (1.0 - sig))).astype(BF16)
    go([ag_copy(d, 0, 0) for d in range(2)])
    gat[1, here, :] = (back * silu).astype(BF16)
    go([ag_copy(d, 0, 1) for d in range(2)])

    def px_copy(k):
        return pltpu.make_async_remote_copy(
            src_ref=pxo.at[k], dst_ref=pxi.at[k], send_sem=pxs.at[k], recv_sem=pxr.at[k],
            device_id=other, device_id_type=MESH,
        )

    def grads(k):
        at = span(z_off(k), chunk)
        val = dot(gat[0, at, :], wg[...], ((1,), (1,))) + dot(gat[1, at, :], wu[...], ((1,), (1,)))
        keep[k] = val
        pxo[k] = keep[k, :, theirs].astype(BF16)
        go([px_copy(k)])

    def piece(k, p):
        at = z_off(k)
        px = (at // n * pieces if nz > n else 0) + p
        peer = px * n + lax.rem(at + px + mx + my, n)
        return peer, pltpu.make_async_remote_copy(
            src_ref=rt.at[k, span(p, room), :], dst_ref=rc.at[span(me, room), :],
            send_sem=hs.at[k * pieces + p], recv_sem=hr.at[me],
            device_id={"expert": peer}, device_id_type=MESH,
        )

    def settle(k):
        px_copy(k).wait_recv()
        val = (keep[k, :, mine] + pxi[k].astype(F32)).astype(BF16)
        rt[k] = dot(pad[...], val).astype(BF16)

        def send(p, _):
            peer, copy = piece(k, p)

            @pl.when(peer != me)
            def _():
                copy.start()

            @pl.when(peer == me)
            def _():
                rc[span(me, room), :] = rt[k, span(p, room), :]

            return 0

        lax.fori_loop(0, pieces, send, 0)

    grads(0)

    p_row = lax.broadcasted_iota(jnp.int32, (pieces * room, 1), 0).astype(F32)
    p_div = jnp.floor((p_row + 0.5) * (1.0 / room))
    p_rank = p_row - p_div * room
    p_lane = lax.broadcasted_iota(jnp.int32, (pieces * room, chunk), 1).astype(F32)
    pad[...] = jnp.where((p_lane == p_div * cap + p_rank) & (p_rank < cap), 1.0, 0.0).astype(BF16)
    h_row = lax.broadcasted_iota(jnp.int32, (ex * room, 1), 0).astype(F32)
    h_exp = jnp.floor((h_row + 0.5) * (1.0 / room))
    h_rank = h_row - h_exp * room
    unfold = (h_exp == lax.broadcasted_iota(jnp.int32, (ex * room, ex), 1).astype(F32)).astype(BF16)
    placed, _ = select(e_row)
    h_hit = (dot(unfold, placed) == h_rank + 1.0) & (h_rank < cap)
    eye = (
        lax.broadcasted_iota(jnp.int32, (tok, tok), 0) == lax.broadcasted_iota(jnp.int32, (tok, tok), 1)
    ).astype(BF16)
    pcomb[...] = dot(eye, jnp.where(h_hit, 1.0, 0.0).astype(BF16), ((1,), (1,))).astype(BF16)

    def forward(s, j):
        for d in range(2):
            ag_arrived(d, s - 1, j)
            if s < half_z:
                go([ag_copy(d, s, j)])

    done = [0]
    for s in range(1, half_z):
        forward(s, 0)
        settle(done[0])
        forward(s, 1)
        grads(s)
        if len(done) > 1:
            settle(done[1])
        forward(s, 2)
        grads(nz - s)
        done = [s, nz - s]
    for k in done:
        settle(k)
    forward(half_z, 0)
    forward(half_z, 1)
    grads(half_z)
    settle(half_z)

    for d in range(2):
        ag_arrived(d, half_z - 1, 2)
    ftile = 256 if hid % 256 == 0 else hid

    def down(f, _):
        cols = span(f, ftile)
        dgrad_ref[cols, :] = dot(gat[2, :, cols], rows[1], ((0,), (0,))).astype(BF16)
        return 0

    lax.fori_loop(0, hid // ftile, down, 0)
    store_dgrad = pltpu.make_async_copy(dgrad_ref, dgrad_hbm, wsem.at[0])
    store_dgrad.start()

    for copy in pending:
        copy.wait_send()

    def sent(i, _):
        k, p = i // pieces, lax.rem(i, pieces)
        peer, copy = piece(k, p)

        @pl.when(peer != me)
        def _():
            copy.wait_send()

        return 0

    lax.fori_loop(0, ex, sent, 0)

    def arrive(e, _):
        @pl.when(e != me)
        def _():
            pltpu.make_async_remote_copy(
                src_ref=rt.at[0, span(0, room), :], dst_ref=rc.at[span(e, room), :],
                send_sem=hs.at[0], recv_sem=hr.at[e],
                device_id={"expert": e}, device_id_type=MESH,
            ).wait_recv()

        return 0

    lax.fori_loop(0, ex, arrive, 0)
    res[:, mine] = dot(pcomb[...], rc[...]).astype(BF16)
    last_swap = pltpu.make_async_remote_copy(
        src_ref=res.at[:, mine], dst_ref=res.at[:, mine], send_sem=fs.at[0], recv_sem=fr.at[0],
        device_id=other, device_id_type=MESH,
    )
    last_swap.start()
    last_swap.wait_recv()
    store_dx = pltpu.make_async_copy(res, dx_hbm, wsem.at[1])
    store_dx.start()
    store_dgrad.wait()
    store_dx.wait()

    last_swap.wait_send()


def hand_out(dx, dgrad, dx_out, dgrad_out, dx_held, dgrad_held, sems):
    part = dgrad.shape[0] // 4
    legs = [(dx, dx_held, dx_out)]
    for i in range(4):
        at = pl.ds(i * part, part)
        legs.append((dgrad.at[at, :], dgrad_held.at[at, :], dgrad_out.at[at, :]))
    into = [pltpu.make_async_copy(src, held, sems.at[0, i]) for i, (src, held, _) in enumerate(legs)]
    out = [pltpu.make_async_copy(held, dst, sems.at[1, i]) for i, (_, held, dst) in enumerate(legs)]
    for copy in into:
        copy.start()
    for first, then in zip(into, out):
        first.wait()
        then.start()
    for copy in out:
        copy.wait()


def body(tokens, cotangent, routes, gates, w_gate, w_up, w_down):
    tok, width = tokens.shape
    top = routes.shape[1]
    hid = w_gate.shape[2]
    experts = lax.axis_size("expert")
    nz = lax.axis_size("dp")
    n = math.isqrt(experts)
    cap = max(2, 5 * tok * top // (4 * experts))
    total = experts * cap
    chunk = total // nz
    hw = width // 2
    hz = nz // 2
    pieces = experts // nz
    room = -(-cap // 16) * 16
    vm = pltpu.VMEM
    dma = pltpu.SemaphoreType.DMA
    in_hbm = pl.BlockSpec(memory_space=pl.ANY)
    scratch = [
        vm((hid, width), BF16),
        vm((top, tok), routes.dtype), vm((top, tok), BF16), vm((tok, width), BF16), vm((tok, width), BF16),
        vm((width, hid), BF16), vm((width, hid), BF16), vm((hid, width), BF16),
        vm((total, total), BF16), vm((total, total), BF16), vm((tok, experts * room), BF16),
        vm((pieces * room, chunk), BF16),
        vm((2, total, hw), BF16), vm((2, total, hw), BF16), vm((2, total, hw), BF16), vm((2, total, hw), BF16),
        vm((2, total, width), BF16),
        vm((3, total, hid), F32),
        vm((3, chunk, hid), BF16),
        vm((2, hz, 3, chunk, hid), BF16),
        vm((3, total, hid), BF16),
        vm((nz, chunk, width), F32),
        vm((nz, chunk, hw), BF16), vm((nz, chunk, hw), BF16),
        vm((nz, pieces * room, hw), BF16), vm((experts * room, hw), BF16),
        vm((tok, width), BF16),
        dma((7,)),
        dma((2, n)), dma((2, n)), dma((2, n)), dma((2, n)),
        dma((2,)), dma((2,)),
        dma((2, hz, 3)), dma((2, hz, 3)), dma((2, hz, 3)), dma((2, hz, 3)),
        dma((nz,)), dma((nz,)),
        dma((experts,)), dma((experts,)),
        dma((1,)), dma((1,)),
    ]
    dx, dgrad = pl.pallas_call(
        functools.partial(kernel, (n, nz, cap, tok, top, width, hid)),
        out_shape=(
            jax.ShapeDtypeStruct((tok, width), BF16),
            jax.ShapeDtypeStruct((hid, width), BF16),
        ),
        in_specs=[in_hbm] * 7,
        out_specs=(in_hbm, in_hbm),
        scratch_shapes=scratch,
        compiler_params=pltpu.CompilerParams(
            collective_id=0, has_side_effects=True, vmem_limit_bytes=62 * 1024 * 1024
        ),
        cost_estimate=pl.CostEstimate(
            flops=12 * total * width * hid, bytes_accessed=8 * width * hid, transcendentals=chunk * hid
        ),
    )(routes.T, gates.T, tokens, cotangent, w_gate[0], w_up[0], w_down[0])
    dx, dgrad = pl.pallas_call(
        hand_out,
        out_shape=(
            jax.ShapeDtypeStruct((tok, width), BF16),
            jax.ShapeDtypeStruct((hid, width), BF16),
        ),
        in_specs=[in_hbm] * 2,
        out_specs=(in_hbm, in_hbm),
        scratch_shapes=[vm((tok, width), BF16), vm((hid, width), BF16), dma((2, 5))],
        compiler_params=pltpu.CompilerParams(vmem_limit_bytes=62 * 1024 * 1024),
        cost_estimate=pl.CostEstimate(
            flops=0, bytes_accessed=4 * width * (hid + tok), transcendentals=0
        ),
    )(dx, dgrad)
    return dx, dgrad[None]


def solution(mesh):
    return jax.shard_map(
        body,
        mesh=mesh,
        in_specs=(
            P("expert", "dp"),
            P("expert", "dp"),
            P("expert", None),
            P("expert", None),
            P("expert", "dp", "tensor"),
            P("expert", "dp", "tensor"),
            P("expert", "tensor", "dp"),
        ),
        out_specs=(P("expert", "dp"), P("expert", "tensor", "dp")),
        check_vma=False,
    )
```
